32 devices in a mesh: row: 4 (over y, x), col: 4 (over z), depth: 2 (over core).
Axes of the slice: x: 2, y: 2, z: 4, core: 2. Of those that a mesh axis runs over, the one named last changes fastest.
Arguments:
- covariance: float32 [12, 4, 12, 4, 256, 256], P(None, 'row', None, 'col'), may hold values from 0 to 2, as said below
Outputs:
- factored: float32 [12, 4, 12, 4, 256, 256], P(None, 'row', None, 'col', 'depth')
The draws below stay inside these ranges and needn't reach their ends.
Inputs may be any that keep to these rules, and one draw needn't show every extreme that they name: covariance is the Matern kernel of smoothness 3/2, (1 + rho) exp(-rho) with rho = sqrt(3) times the scaled distance, over 12288 points in the unit cube of 8 coordinates with length scales between 0.3 and 1.2, plus a nugget between 0.2 and 1 on the diagonal; it is symmetric positive definite.
All inputs are finite; a program needn't handle non-finite values.
Results may differ from the reference program's by a relative error of at most 0.0003.
Values sent between devices are 32-bit elements; how exact they have to be, the bound alone decides.
No kernel may reach another device: no remote copies, remote signals or barrier semaphores. Data moves between devices by JAX's collectives and lax.ppermute only.
A program may use at most 192 MiB of HBM per device.

```python
import math
import jax
import jax.numpy as jnp
from jax import lax

ORDER = 12288
TILE = 256
DIMS = 8
STEPS = 1
N_ROW = 4
N_COL = 4


def draw_covariance(key, part):
    point_key = jax.random.fold_in(key, 11)
    scale_key = jax.random.fold_in(key, 12)
    nugget_key = jax.random.fold_in(key, 13)
    design = jax.random.uniform(point_key, (DIMS, ORDER), jnp.float32)
    scales = jnp.exp(jax.random.uniform(scale_key, (DIMS,), jnp.float32, math.log(0.3), math.log(1.2)))
    nugget = jnp.exp(jax.random.uniform(nugget_key, (), jnp.float32, math.log(0.2), math.log(1.0)))
    squared = jnp.zeros((ORDER, ORDER), jnp.float32)
    for dim_index in range(DIMS):
        offset = (design[dim_index][:, None] - design[dim_index][None, :]) / scales[dim_index]
        squared = squared + offset * offset
    radius = jnp.sqrt(squared + 1e-12) * math.sqrt(3.0)
    matrix = (1.0 + radius) * jnp.exp(-radius) + nugget * jnp.eye(ORDER, dtype=jnp.float32)
    tile_rows = ORDER // TILE // N_ROW
    tile_cols = ORDER // TILE // N_COL
    return matrix.reshape(tile_rows, N_ROW, TILE, tile_cols, N_COL, TILE).transpose(0, 1, 3, 4, 2, 5)


def setup_inputs(seed: int = 0) -> dict:
    splits = jax.random.split(jax.random.key(seed), 2)
    covariance = draw_covariance(jax.random.fold_in(splits[1], 71), 0)
    return dict(covariance=covariance)


def reference(covariance):
    panel_width = 2 * TILE
    matrix = covariance.transpose(0, 1, 4, 2, 3, 5).reshape(ORDER, ORDER)
    factors = []
    for panel_step in range(STEPS):
        first_row = panel_step * panel_width
        last_row = first_row + panel_width
        factor_lower = jnp.linalg.cholesky(matrix[first_row:last_row, first_row:last_row])
        solved = jax.scipy.linalg.solve_triangular(factor_lower, matrix[first_row:, first_row:last_row].T, lower=True).T
        factors.append(solved)
        below_rows = solved[panel_width:]
        update = jnp.dot(below_rows, below_rows.T, precision=lax.Precision.HIGHEST)
        matrix = matrix.at[last_row:, last_row:].add(-update)
    factored_width = STEPS * panel_width
    result = matrix.at[:, :factored_width].set(0.0).at[:factored_width, factored_width:].set(0.0)
    for panel_step in range(STEPS):
        first_row = panel_step * panel_width
        result = result.at[first_row:, first_row:first_row + panel_width].set(factors[panel_step])
    tile_rows = ORDER // TILE // N_ROW
    tile_cols = ORDER // TILE // N_COL
    return result.reshape(tile_rows, N_ROW, TILE, tile_cols, N_COL, TILE).transpose(0, 1, 3, 4, 2, 5)
```

```python
import functools

import jax
import jax.numpy as jnp
from jax import lax
from jax.experimental import pallas as pl
from jax.experimental.pallas import tpu as pltpu
from jax.sharding import PartitionSpec as P

EXACT = lax.Precision.HIGHEST
F32 = jnp.float32
BF16 = jnp.bfloat16
LIMIT = 56 << 20
ANY = pl.BlockSpec(memory_space=pl.ANY)
LIGHT = pl.CostEstimate(flops=1, bytes_accessed=1, transcendentals=0)


def dot(a, b, ca=1, cb=0, precision=None):
    return lax.dot_general(
        a, b, (((ca,), (cb,)), ((), ())), precision=precision, preferred_element_type=F32
    )


def split(value):
    high = value.astype(BF16)
    return high, (value - high.astype(F32)).astype(BF16)


def diag_inverse(block, n, group=8):
    row_ids = lax.broadcasted_iota(jnp.int32, (n, n), 0)
    col_ids = lax.broadcasted_iota(jnp.int32, (n, n), 1)
    unit = jnp.where(row_ids == col_ids, 1.0, 0.0).astype(F32)
    sub = lax.broadcasted_iota(jnp.int32, (group, n), 0)
    count = n // group
    rows = [block[group * g : group * (g + 1)] for g in range(count)]
    inverse = [unit[group * g : group * (g + 1)] for g in range(count)]

    def lanes(value, index):
        return jnp.broadcast_to(value[:, index : index + 1], (group, n))

    def subs(value, index):
        return jnp.broadcast_to(value[index : index + 1], (group, n))

    done = []
    for g in range(count):
        first = group * g
        here, inv_here = rows[g], inverse[g]
        cols = [lanes(here, first + j) for j in range(group)]
        recips, pivots, inv_pivots, cross = [], [], [], {}
        scale = jnp.zeros((group, n), F32)
        for j in range(group):
            root = lax.rsqrt(subs(cols[j], j))
            recip = root * root
            scale = jnp.where(sub == j, root, scale)
            pivot, inv_pivot = subs(here, j), subs(inv_here, j)
            factor = jnp.where(sub > j, cols[j] * recip, 0.0)
            for later in range(j + 1, group):
                cross[j, later] = subs(cols[later], j)
                cols[later] = cols[later] - factor * cross[j, later]
            here = here - factor * pivot
            inv_here = inv_here - factor * inv_pivot
            recips.append(recip)
            pivots.append(pivot)
            inv_pivots.append(inv_pivot)
        done.append(inv_here * scale)
        for below in range(g + 1, count):
            value, inv_value = rows[below], inverse[below]
            cols = [lanes(value, first + j) for j in range(group)]
            for j in range(group):
                factor = cols[j] * recips[j]
                for later in range(j + 1, group):
                    cols[later] = cols[later] - factor * cross[j, later]
                value = value - factor * pivots[j]
                inv_value = inv_value - factor * inv_pivots[j]
            rows[below], inverse[below] = value, inv_value
    return jnp.concatenate(done, 0)


def factor_steps(matrix, out, start, stop, step):
    n = matrix.shape[0]
    for a in range(start, stop, step):
        e = a + step
        inv = diag_inverse(matrix[a:e, a:e], step)
        if a:
            out[a:e, :a] = dot(inv, out[a:e, :a], precision=EXACT)
        out[a:e, a:e] = inv
        if e < n:
            panel = dot(inv, matrix[a:e, e:], precision=EXACT)
            matrix[e:, e:] = matrix[e:, e:] - dot(panel, panel, 0, 0, EXACT)
            out[e:, :e] = out[e:, :e] - dot(panel, out[a:e, :e], 0, 0, EXACT)


def assemble_kernel(place, mine, across, mine_other, across_other, matrix, out, *, step):
    half = mine.shape[1]
    tile = mine.shape[2]
    parity = lax.rem(place[0], 2)
    depth = place[2]
    for ref, tile_row, side in (
        (mine, parity, depth),
        (across, 1 - parity, depth),
        (mine_other, parity, 1 - depth),
        (across_other, 1 - parity, 1 - depth),
    ):
        start = pl.multiple_of(tile_row * tile + side * half, half)
        for q in range(2):
            matrix[pl.ds(start, half), q * tile : (q + 1) * tile] = ref[q]
    out[...] = jnp.zeros_like(out)
    factor_steps(matrix, out, 0, step, step)


def eliminate_kernel(matrix_in, inv_in, matrix, inv, *, start, stop, step):
    matrix[...] = matrix_in[...]
    inv[...] = inv_in[...]
    factor_steps(matrix, inv, start, stop, step)


def factor_start(place, pieces, step):
    n = 2 * pieces[0].shape[-1]
    whole = pl.BlockSpec(memory_space=pltpu.VMEM)
    square = jax.ShapeDtypeStruct((n, n), F32)
    return pl.pallas_call(
        functools.partial(assemble_kernel, step=step),
        out_shape=[square, square],
        in_specs=[pl.BlockSpec(memory_space=pltpu.SMEM)] + [whole] * 4,
        out_specs=[whole] * 2,
        compiler_params=pltpu.CompilerParams(vmem_limit_bytes=16 << 20),
        cost_estimate=LIGHT,
        name="factor_start",
    )(place, *pieces)


def factor_next(matrix, inv, start, stop, step):
    n = matrix.shape[0]
    whole = pl.BlockSpec(memory_space=pltpu.VMEM)
    square = jax.ShapeDtypeStruct((n, n), F32)
    return pl.pallas_call(
        functools.partial(eliminate_kernel, start=start, stop=stop, step=step),
        out_shape=[square, square],
        in_specs=[whole] * 2,
        out_specs=[whole] * 2,
        compiler_params=pltpu.CompilerParams(vmem_limit_bytes=16 << 20),
        cost_estimate=LIGHT,
        name="factor_next",
    )(matrix, inv)


def columns_kernel(place, inv, *refs, parts):
    both_parts, first, raw = refs[-3:]
    group, half, tile = refs[0].shape
    n = 2 * tile
    parity = lax.rem(place[0], 2)
    depth = place[2]
    turn = pl.program_id(0) // (pl.num_programs(0) // parts)
    sides = ((parity, depth), (1 - parity, depth), (parity, 1 - depth), (1 - parity, 1 - depth))

    for part in range(parts):

        @pl.when(turn == part)
        def _(part=part):
            for ref, (q, side) in zip(refs[4 * part : 4 * part + 4], sides):
                start = pl.multiple_of(q * tile + side * half, half)
                for b in range(group):
                    raw[pl.ds(start, half), b * tile : (b + 1) * tile] = ref[b]

    for b in range(group):
        here = slice(b * tile, (b + 1) * tile)
        for start, stop in ((0, tile), (tile, n)):
            total = dot(inv[start:stop, :stop], raw[:stop, here], precision=EXACT)
            if start == 0:
                first[:, here] = jnp.broadcast_to(total[:1], (8, tile))
                total = jnp.where(lax.broadcasted_iota(jnp.int32, total.shape, 0) == 0, 0.0, total)
            high, low = split(total)
            both_parts[start:stop, here] = high
            both_parts[n + start : n + stop, here] = low


def columns(place, inv, pieces, parts, group):
    count, half, tile = pieces[0].shape
    n = 2 * tile
    steps = count // group
    width = group * tile

    def piece(part):
        return pl.BlockSpec(
            (group, half, tile), lambda j, place: (jnp.clip(j - part * steps, 0, steps - 1), 0, 0)
        )

    return pl.pallas_call(
        functools.partial(columns_kernel, parts=parts),
        out_shape=[
            jax.ShapeDtypeStruct((2 * n, parts * count * tile), BF16),
            jax.ShapeDtypeStruct((8, parts * count * tile), F32),
        ],
        grid_spec=pltpu.PrefetchScalarGridSpec(
            num_scalar_prefetch=1,
            grid=(parts * steps,),
            in_specs=[pl.BlockSpec((n, n), lambda j, place: (0, 0))]
            + [piece(number // 4) for number in range(len(pieces))],
            out_specs=[
                pl.BlockSpec((2 * n, width), lambda j, place: (0, j)),
                pl.BlockSpec((8, width), lambda j, place: (0, j)),
            ],
            scratch_shapes=[pltpu.VMEM((n, width), F32)],
        ),
        compiler_params=pltpu.CompilerParams(vmem_limit_bytes=LIMIT),
        cost_estimate=LIGHT,
        name="columns",
    )(place, inv, *pieces)


def update_kernel(place, inv, *refs, sources, plan, first_tile):
    cands = refs[:sources]
    top, top_first, tiles = refs[sources : sources + 3]
    out, raw, exact, lead, high, low = refs[-6:]
    chunk_rows, _, group, _, half, tile = out.shape
    n = 2 * tile
    step = pl.program_id(0)
    row, col = place[0], place[1]

    @pl.when(step == 0)
    def _():
        for number, offset, at_first, at_second, begin, size in plan:
            ref = cands[number]
            place_rows = slice(begin * half, (begin + size) * half)
            for at, lanes in ((at_first, slice(0, tile)), (at_second, slice(tile, n))):
                here = functools.reduce(jnp.logical_or, [col == index for index in at])

                @pl.when(here)
                def _(ref=ref, lanes=lanes, place_rows=place_rows, offset=offset, size=size):
                    raw[place_rows, lanes] = ref[offset : offset + size].reshape(size * half, tile)

        for start, stop in ((0, tile), (tile, n)):
            total = dot(raw[:, :stop], inv[start:stop, :stop], 1, 1, EXACT)
            exact[:, start:stop] = total
            if start == 0:
                lead[...] = jnp.broadcast_to(total[:, :1], lead.shape)
            high[:, start:stop], low[:, start:stop] = split(total)

    leads = jnp.concatenate([lead[...]] * (tile // 128), 1)
    for b in range(group):
        here = slice(b * tile, (b + 1) * tile)
        total = dot(high[...], top[:n, here])
        total += dot(high[...], top[n:, here])
        total += dot(low[...], top[:n, here])
        total += leads * top_first[:1, here]
        for a in range(chunk_rows):
            out[a, 0, b, 0] = tiles[a, 0, b, 0] - total[a * half : (a + 1) * half]

    @pl.when(jnp.logical_and(first_tile == 0, row < 2))
    def _():
        out[0] = jnp.zeros(out.shape[1:], F32)

    @pl.when(jnp.logical_and(step == 0, col < 2))
    def _():
        start = pl.multiple_of(jnp.minimum(col, 1) * tile, tile)
        panel = exact[:, pl.ds(start, tile)]
        for a in range(chunk_rows):
            out[a, 0, 0, 0] = panel[a * half : (a + 1) * half]


def update(place, inv, groups, top, covariance, before, first_tile, group):
    tile_rows, _, tile_cols, _, tile, _ = covariance.shape
    half = tile // 2
    n = 2 * tile
    cands, plan = [], []
    begin = 0
    for size, parts in groups:
        for array, offset, at_first, at_second in parts:
            number = next((i for i, known in enumerate(cands) if known is array), len(cands))
            if number == len(cands):
                cands.append(array)
            plan.append((number, offset, at_first, at_second, begin, size))
        begin += size
    chunk_rows = begin
    rows = chunk_rows * half
    width = group * tile
    chunk = first_tile // chunk_rows
    in_specs = [pl.BlockSpec((n, n), lambda j, place: (0, 0))]
    in_specs += [pl.BlockSpec(array.shape, lambda j, place: (0, 0, 0)) for array in cands]
    in_specs += [
        pl.BlockSpec((2 * n, width), lambda j, place: (0, j)),
        pl.BlockSpec((8, width), lambda j, place: (0, j)),
        pl.BlockSpec(
            (chunk_rows, 1, group, 1, half, tile),
            lambda j, place: (chunk, 0, j, 0, place[2], 0),
        ),
    ]
    operands = [place, inv, *cands, *top, covariance]
    aliases = {}
    if before is not None:
        in_specs.append(ANY)
        aliases = {len(operands): 0}
        operands.append(before)
    return pl.pallas_call(
        functools.partial(update_kernel, sources=len(cands), plan=plan, first_tile=first_tile),
        out_shape=jax.ShapeDtypeStruct((tile_rows, 1, tile_cols, 1, half, tile), F32),
        grid_spec=pltpu.PrefetchScalarGridSpec(
            num_scalar_prefetch=1,
            grid=(tile_cols // group,),
            in_specs=in_specs,
            out_specs=pl.BlockSpec(
                (chunk_rows, 1, group, 1, half, tile), lambda j, place: (chunk, 0, j, 0, 0, 0)
            ),
            scratch_shapes=[
                pltpu.VMEM((rows, n), F32),
                pltpu.VMEM((rows, n), F32),
                pltpu.VMEM((rows, 128), F32),
                pltpu.VMEM((rows, n), BF16),
                pltpu.VMEM((rows, n), BF16),
            ],
        ),
        input_output_aliases=aliases,
        compiler_params=pltpu.CompilerParams(vmem_limit_bytes=LIMIT),
        cost_estimate=pl.CostEstimate(
            flops=12 * rows * n * tile_cols * tile,
            bytes_accessed=8 * rows * tile_cols * tile,
            transcendentals=0,
        ),
        name="update",
    )(*operands)


def after(value, *earlier):
    return lax.optimization_barrier((value, *earlier))[0] if earlier else value


def outward(value, axis, turn=0):
    return lax.ppermute(value, axis, [(0, 3), (1, 2)] if turn else [(0, 2), (1, 3)])


def exchange(value, axis, pairs):
    return lax.ppermute(value, axis, pairs + [(j, i) for i, j in pairs])


def held_and_across(value, axis, size):
    held = value
    index = lax.axis_index(axis)
    step = 2
    while step < size:
        pairs = [(i, i + step) for i in range(step) if i + step < size]
        got = lax.ppermute(held, axis, pairs)
        held = jnp.where((index >= step) & (index < 2 * step), got, held)
        step *= 2
    return held, lax.ppermute(held, axis, [(i, i ^ 1) for i in range(size)])


def pick(parts, side, index):
    value = parts[-1][0]
    for array, _, *at in parts[:-1]:
        here = functools.reduce(jnp.logical_or, [index == position for position in at[side]])
        value = jnp.where(here, array, value)
    return value


def spread(value, index, size):
    held = value
    step = 2
    while step < size:
        pairs = [(i, i + step) for i in range(step) if i + step < size]
        got = lax.ppermute(held, "row", pairs)
        held = jnp.where((index >= step) & (index < 2 * step), got, held)
        step *= 2
    return held


def cross(value, size):
    return lax.ppermute(value, "row", [(i, i ^ 1) for i in range(size)])


def swap(value):
    return lax.ppermute(value, "depth", [(0, 1), (1, 0)])


def divisor(count, wanted):
    while count % wanted:
        wanted -= 1
    return wanted


def piece_sizes(count):
    if count == 12:
        return [1, 2, 3, 3, 3], [(0, 3), (3, 5)]
    return ([1, count - 1] if count > 1 else [1]), [(0, 2)]


def parts_of(own, swapped, offset, gone, back, turn):
    far = [((2,), (3,)), ((3,), (2,))]
    if turn:
        far.reverse()
    return [(own, 0, (0,), (1,)), (swapped, offset, (1,), (0,)), (gone, 0, *far[0]), (back, 0, *far[1])]


def plain_parts(arrays, size):
    even, odd = tuple(range(0, size, 2)), tuple(range(1, size, 2))
    return [(arrays[0], 0, even, odd), (arrays[1], 0, odd, even)]


def on_device(covariance):
    rows = lax.axis_size("row")
    cols = lax.axis_size("col")
    row, col, depth = (lax.axis_index(name) for name in ("row", "col", "depth"))
    place = jnp.stack([row, col, depth]).astype(jnp.int32)
    tile_rows, _, tile_cols, _, tile, _ = covariance.shape
    half = tile // 2
    zero = jnp.zeros((), jnp.int32)
    start = depth.astype(jnp.int32) * half

    def left(first, count):
        where = (zero + first, zero, zero, zero, start, zero)
        return lax.dynamic_slice(covariance, where, (count, 1, 1, 1, half, tile)).reshape(count, half, tile)

    def top(first, count):
        where = (zero, zero, zero + first, zero, start, zero)
        return lax.dynamic_slice(covariance, where, (1, 1, count, 1, half, tile)).reshape(count, half, tile)

    sizes, groups_at = piece_sizes(tile_rows)
    tall = cols == 4 and len(sizes) == 5
    mine = [left(sum(sizes[:i]), size) for i, size in enumerate(sizes)]
    turns = [i % 2 for i in range(len(sizes))]
    pairs = [(0, 1)], [(2, 3)]
    if tall:
        gone = [outward(mine[0], "col")]
        first_parts = parts_of(mine[0], exchange(mine[0], "col", pairs[0]), 0, gone[0], exchange(gone[0], "col", pairs[1]), 0)
        rest = left(1, tile_rows - 1)
    else:
        first_parts = plain_parts(held_and_across(mine[0], "col", cols), cols)

    top_parts = 3 if tile_cols % 3 == 0 else 1
    per_part = tile_cols // top_parts
    tops_held = [spread(top(0, per_part), row, rows)]
    pair = jnp.concatenate([pick(first_parts, side, col) for side in range(2)], 0)
    seed = spread(after(pair, tops_held[0]), row, rows)
    for part in range(1, top_parts):
        tops_held.append(spread(after(top(part * per_part, per_part), seed), row, rows))
    seed_across = cross(seed, rows)
    tops_across = [cross(after(tops_held[0], seed_across), rows)]
    seed_parts = [seed, seed_across, swap(seed), swap(seed_across)]
    if tall:
        gone.append(outward(after(mine[1], pair), "col", turns[1]))
        gone.append(outward(after(mine[2], seed), "col", turns[2]))
        seed_parts[3] = after(seed_parts[3], gone[1])
    matrix, inv = factor_start(place, seed_parts, half)
    stages = [matrix]
    for number, (begin, end) in enumerate(((half, tile), (tile, 2 * tile))):
        if tall:
            gone.append(outward(after(mine[3 + number], stages[number]), "col", turns[3 + number]))
            if number:
                matrix = after(matrix, gone[2])
        matrix, inv = factor_next(matrix, inv, begin, end, half)
        stages.append(matrix)
    for part in range(1, top_parts):
        tops_across.append(cross(after(tops_held[part], stages[part - 1]), rows))
    pieces = []
    for part in range(top_parts):
        waits = stages[min(part, 2)]
        pieces += [
            tops_held[part],
            tops_across[part],
            swap(after(tops_held[part], waits)),
            swap(after(tops_across[part], waits)),
        ]
    if tall:
        pieces[0] = after(pieces[0], gone[3])
    tops = columns(place, inv, pieces, top_parts, divisor(per_part, 2))

    groups = [(sizes[0], first_parts)]
    if tall:
        swapped = exchange(after(rest, stages[0]), "col", pairs[0])
        starts = (stages[0], stages[2], tops[1], gone[4])
        for number in range(1, len(sizes)):
            back = exchange(after(gone[number], starts[number - 1]), "col", pairs[1])
            offset = sum(sizes[1:number])
            own = after(mine[number], gone[4]) if number == 1 else mine[number]
            groups.append(
                (sizes[number], parts_of(own, swapped, offset, gone[number], back, turns[number]))
            )
    else:
        for number in range(1, len(sizes)):
            groups.append((sizes[number], plain_parts(held_and_across(mine[number], "col", cols), cols)))

    out = None
    group = divisor(tile_cols, 3)
    for begin, end in groups_at:
        first_tile = sum(sizes[:begin])
        out = update(place, inv, groups[begin:end], tops, covariance, out, first_tile, group)
    return out


def solution(mesh):
    in_specs = (P(None, "row", None, "col", None, None),)
    out_specs = P(None, "row", None, "col", "depth", None)
    return jax.shard_map(
        on_device, mesh=mesh, in_specs=in_specs, out_specs=out_specs, check_vma=False
    )
```

```python
import functools

import jax
import jax.numpy as jnp
from jax import lax
from jax.experimental import pallas as pl
from jax.experimental.pallas import tpu as pltpu
from jax.sharding import PartitionSpec as P

EXACT = lax.Precision.HIGHEST
F32 = jnp.float32
BF16 = jnp.bfloat16
LIMIT = 56 << 20
ANY = pl.BlockSpec(memory_space=pl.ANY)
LIGHT = pl.CostEstimate(flops=1, bytes_accessed=1, transcendentals=0)
HEAVY = pl.CostEstimate(flops=10**10, bytes_accessed=1, transcendentals=0)


def dot(a, b, ca=1, cb=0, precision=None):
    return lax.dot_general(
        a, b, (((ca,), (cb,)), ((), ())), precision=precision, preferred_element_type=F32
    )


def split(value):
    high = value.astype(BF16)
    return high, (value - high.astype(F32)).astype(BF16)


def diag_inverse(block, n, group=8):
    row_ids = lax.broadcasted_iota(jnp.int32, (n, n), 0)
    col_ids = lax.broadcasted_iota(jnp.int32, (n, n), 1)
    unit = jnp.where(row_ids == col_ids, 1.0, 0.0).astype(F32)
    sub = lax.broadcasted_iota(jnp.int32, (group, n), 0)
    count = n // group
    rows = [block[group * g : group * (g + 1)] for g in range(count)]
    inverse = [unit[group * g : group * (g + 1)] for g in range(count)]

    def lanes(value, index):
        return jnp.broadcast_to(value[:, index : index + 1], (group, n))

    def subs(value, index):
        return jnp.broadcast_to(value[index : index + 1], (group, n))

    done = []
    for g in range(count):
        first = group * g
        here, inv_here = rows[g], inverse[g]
        cols = [lanes(here, first + j) for j in range(group)]
        recips, pivots, inv_pivots, cross = [], [], [], {}
        scale = jnp.zeros((group, n), F32)
        for j in range(group):
            root = lax.rsqrt(subs(cols[j], j))
            recip = root * root
            scale = jnp.where(sub == j, root, scale)
            pivot, inv_pivot = subs(here, j), subs(inv_here, j)
            factor = jnp.where(sub > j, cols[j] * recip, 0.0)
            for later in range(j + 1, group):
                cross[j, later] = subs(cols[later], j)
                cols[later] = cols[later] - factor * cross[j, later]
            here = here - factor * pivot
            inv_here = inv_here - factor * inv_pivot
            recips.append(recip)
            pivots.append(pivot)
            inv_pivots.append(inv_pivot)
        done.append(inv_here * scale)
        for below in range(g + 1, count):
            value, inv_value = rows[below], inverse[below]
            cols = [lanes(value, first + j) for j in range(group)]
            for j in range(group):
                factor = cols[j] * recips[j]
                for later in range(j + 1, group):
                    cols[later] = cols[later] - factor * cross[j, later]
                value = value - factor * pivots[j]
                inv_value = inv_value - factor * inv_pivots[j]
            rows[below], inverse[below] = value, inv_value
    return jnp.concatenate(done, 0)


def factor_steps(matrix, out, start, stop, step):
    n = matrix.shape[0]
    for a in range(start, stop, step):
        e = a + step
        inv = diag_inverse(matrix[a:e, a:e], step)
        if a:
            out[a:e, :a] = dot(inv, out[a:e, :a], precision=EXACT)
        out[a:e, a:e] = inv
        if e < n:
            panel = dot(inv, matrix[a:e, e:], precision=EXACT)
            matrix[e:, e:] = matrix[e:, e:] - dot(panel, panel, 0, 0, EXACT)
            out[e:, :e] = out[e:, :e] - dot(panel, out[a:e, :e], 0, 0, EXACT)


def assemble_kernel(place, mine, across, mine_other, across_other, matrix, out, *, step):
    half = mine.shape[1]
    tile = mine.shape[2]
    parity = lax.rem(place[0], 2)
    depth = place[2]
    for ref, tile_row, side in (
        (mine, parity, depth),
        (across, 1 - parity, depth),
        (mine_other, parity, 1 - depth),
        (across_other, 1 - parity, 1 - depth),
    ):
        start = pl.multiple_of(tile_row * tile + side * half, half)
        for q in range(2):
            matrix[pl.ds(start, half), q * tile : (q + 1) * tile] = ref[q]
    out[...] = jnp.zeros_like(out)
    factor_steps(matrix, out, 0, step, step)


def eliminate_kernel(matrix_in, inv_in, matrix, inv, *, start, stop, step):
    matrix[...] = matrix_in[...]
    inv[...] = inv_in[...]
    factor_steps(matrix, inv, start, stop, step)


def factor_start(place, pieces, step):
    n = 2 * pieces[0].shape[-1]
    whole = pl.BlockSpec(memory_space=pltpu.VMEM)
    square = jax.ShapeDtypeStruct((n, n), F32)
    return pl.pallas_call(
        functools.partial(assemble_kernel, step=step),
        out_shape=[square, square],
        in_specs=[pl.BlockSpec(memory_space=pltpu.SMEM)] + [whole] * 4,
        out_specs=[whole] * 2,
        compiler_params=pltpu.CompilerParams(vmem_limit_bytes=16 << 20),
        cost_estimate=LIGHT,
        name="factor_start",
    )(place, *pieces)


def factor_next(matrix, inv, start, stop, step):
    n = matrix.shape[0]
    whole = pl.BlockSpec(memory_space=pltpu.VMEM)
    square = jax.ShapeDtypeStruct((n, n), F32)
    return pl.pallas_call(
        functools.partial(eliminate_kernel, start=start, stop=stop, step=step),
        out_shape=[square, square],
        in_specs=[whole] * 2,
        out_specs=[whole] * 2,
        compiler_params=pltpu.CompilerParams(vmem_limit_bytes=16 << 20),
        cost_estimate=HEAVY if stop == n else LIGHT,
        name="factor_next",
    )(matrix, inv)


def columns_kernel(place, inv, *refs, parts):
    both_parts, first, raw = refs[-3:]
    group, half, tile = refs[0].shape
    n = 2 * tile
    parity = lax.rem(place[0], 2)
    depth = place[2]
    turn = pl.program_id(0) // (pl.num_programs(0) // parts)
    sides = ((parity, depth), (1 - parity, depth), (parity, 1 - depth), (1 - parity, 1 - depth))

    for part in range(parts):

        @pl.when(turn == part)
        def _(part=part):
            for ref, (q, side) in zip(refs[4 * part : 4 * part + 4], sides):
                start = pl.multiple_of(q * tile + side * half, half)
                for b in range(group):
                    raw[pl.ds(start, half), b * tile : (b + 1) * tile] = ref[b]

    for b in range(group):
        here = slice(b * tile, (b + 1) * tile)
        for start, stop in ((0, tile), (tile, n)):
            total = dot(inv[start:stop, :stop], raw[:stop, here], precision=EXACT)
            if start == 0:
                first[:, here] = jnp.broadcast_to(total[:1], (8, tile))
                total = jnp.where(lax.broadcasted_iota(jnp.int32, total.shape, 0) == 0, 0.0, total)
            high, low = split(total)
            both_parts[start:stop, here] = high
            both_parts[n + start : n + stop, here] = low


def columns(place, inv, pieces, parts, group):
    count, half, tile = pieces[0].shape
    n = 2 * tile
    steps = count // group
    width = group * tile

    def piece(part):
        return pl.BlockSpec(
            (group, half, tile), lambda j, place: (jnp.clip(j - part * steps, 0, steps - 1), 0, 0)
        )

    return pl.pallas_call(
        functools.partial(columns_kernel, parts=parts),
        out_shape=[
            jax.ShapeDtypeStruct((2 * n, parts * count * tile), BF16),
            jax.ShapeDtypeStruct((8, parts * count * tile), F32),
        ],
        grid_spec=pltpu.PrefetchScalarGridSpec(
            num_scalar_prefetch=1,
            grid=(parts * steps,),
            in_specs=[pl.BlockSpec((n, n), lambda j, place: (0, 0))]
            + [piece(number // 4) for number in range(len(pieces))],
            out_specs=[
                pl.BlockSpec((2 * n, width), lambda j, place: (0, j)),
                pl.BlockSpec((8, width), lambda j, place: (0, j)),
            ],
            scratch_shapes=[pltpu.VMEM((n, width), F32)],
        ),
        compiler_params=pltpu.CompilerParams(vmem_limit_bytes=LIMIT),
        cost_estimate=HEAVY,
        name="columns",
    )(place, inv, *pieces)


def update_kernel(place, inv, *refs, sources, plan, first_tile):
    cands = refs[:sources]
    top, top_first, tiles = refs[sources : sources + 3]
    out, raw, exact, lead, high, low = refs[-6:]
    chunk_rows, _, group, _, half, tile = out.shape
    n = 2 * tile
    step = pl.program_id(0)
    row, col = place[0], place[1]

    @pl.when(step == 0)
    def _():
        for number, offset, at_first, at_second, begin, size in plan:
            ref = cands[number]
            place_rows = slice(begin * half, (begin + size) * half)
            for at, lanes in ((at_first, slice(0, tile)), (at_second, slice(tile, n))):
                here = functools.reduce(jnp.logical_or, [col == index for index in at])

                @pl.when(here)
                def _(ref=ref, lanes=lanes, place_rows=place_rows, offset=offset, size=size):
                    raw[place_rows, lanes] = ref[offset : offset + size].reshape(size * half, tile)

        for start, stop in ((0, tile), (tile, n)):
            total = dot(raw[:, :stop], inv[start:stop, :stop], 1, 1, EXACT)
            exact[:, start:stop] = total
            if start == 0:
                lead[...] = jnp.broadcast_to(total[:, :1], lead.shape)
            high[:, start:stop], low[:, start:stop] = split(total)

    leads = jnp.concatenate([lead[...]] * (tile // 128), 1)
    for b in range(group):
        here = slice(b * tile, (b + 1) * tile)
        total = dot(high[...], top[:n, here])
        total += dot(high[...], top[n:, here])
        total += dot(low[...], top[:n, here])
        total += leads * top_first[:1, here]
        for a in range(chunk_rows):
            out[a, 0, b, 0] = tiles[a, 0, b, 0] - total[a * half : (a + 1) * half]

    @pl.when(jnp.logical_and(first_tile == 0, row < 2))
    def _():
        out[0] = jnp.zeros(out.shape[1:], F32)

    @pl.when(jnp.logical_and(step == 0, col < 2))
    def _():
        start = pl.multiple_of(jnp.minimum(col, 1) * tile, tile)
        panel = exact[:, pl.ds(start, tile)]
        for a in range(chunk_rows):
            out[a, 0, 0, 0] = panel[a * half : (a + 1) * half]


def update(place, inv, groups, top, covariance, before, first_tile, group):
    tile_rows, _, tile_cols, _, tile, _ = covariance.shape
    half = tile // 2
    n = 2 * tile
    cands, plan = [], []
    begin = 0
    for size, parts in groups:
        for array, offset, at_first, at_second in parts:
            number = next((i for i, known in enumerate(cands) if known is array), len(cands))
            if number == len(cands):
                cands.append(array)
            plan.append((number, offset, at_first, at_second, begin, size))
        begin += size
    chunk_rows = begin
    rows = chunk_rows * half
    width = group * tile
    chunk = first_tile // chunk_rows
    in_specs = [pl.BlockSpec((n, n), lambda j, place: (0, 0))]
    in_specs += [pl.BlockSpec(array.shape, lambda j, place: (0, 0, 0)) for array in cands]
    in_specs += [
        pl.BlockSpec((2 * n, width), lambda j, place: (0, j)),
        pl.BlockSpec((8, width), lambda j, place: (0, j)),
        pl.BlockSpec(
            (chunk_rows, 1, group, 1, half, tile),
            lambda j, place: (chunk, 0, j, 0, place[2], 0),
        ),
    ]
    operands = [place, inv, *cands, *top, covariance]
    aliases = {}
    if before is not None:
        in_specs.append(ANY)
        aliases = {len(operands): 0}
        operands.append(before)
    return pl.pallas_call(
        functools.partial(update_kernel, sources=len(cands), plan=plan, first_tile=first_tile),
        out_shape=jax.ShapeDtypeStruct((tile_rows, 1, tile_cols, 1, half, tile), F32),
        grid_spec=pltpu.PrefetchScalarGridSpec(
            num_scalar_prefetch=1,
            grid=(tile_cols // group,),
            in_specs=in_specs,
            out_specs=pl.BlockSpec(
                (chunk_rows, 1, group, 1, half, tile), lambda j, place: (chunk, 0, j, 0, 0, 0)
            ),
            scratch_shapes=[
                pltpu.VMEM((rows, n), F32),
                pltpu.VMEM((rows, n), F32),
                pltpu.VMEM((rows, 128), F32),
                pltpu.VMEM((rows, n), BF16),
                pltpu.VMEM((rows, n), BF16),
            ],
        ),
        input_output_aliases=aliases,
        compiler_params=pltpu.CompilerParams(vmem_limit_bytes=LIMIT),
        cost_estimate=pl.CostEstimate(
            flops=12 * rows * n * tile_cols * tile,
            bytes_accessed=8 * rows * tile_cols * tile,
            transcendentals=0,
        ),
        name="update",
    )(*operands)


def after(value, *earlier):
    return lax.optimization_barrier((value, *earlier))[0] if earlier else value


def outward(value, axis, turn=0):
    return lax.ppermute(value, axis, [(0, 3), (1, 2)] if turn else [(0, 2), (1, 3)])


def exchange(value, axis, pairs):
    return lax.ppermute(value, axis, pairs + [(j, i) for i, j in pairs])


def held_and_across(value, axis, size):
    held = value
    index = lax.axis_index(axis)
    step = 2
    while step < size:
        pairs = [(i, i + step) for i in range(step) if i + step < size]
        got = lax.ppermute(held, axis, pairs)
        held = jnp.where((index >= step) & (index < 2 * step), got, held)
        step *= 2
    return held, lax.ppermute(held, axis, [(i, i ^ 1) for i in range(size)])


def pick(parts, side, index):
    value = parts[-1][0]
    for array, _, *at in parts[:-1]:
        here = functools.reduce(jnp.logical_or, [index == position for position in at[side]])
        value = jnp.where(here, array, value)
    return value


def spread(value, index, size):
    held = value
    step = 2
    while step < size:
        pairs = [(i, i + step) for i in range(step) if i + step < size]
        got = lax.ppermute(held, "row", pairs)
        held = jnp.where((index >= step) & (index < 2 * step), got, held)
        step *= 2
    return held


def cross(value, size):
    return lax.ppermute(value, "row", [(i, i ^ 1) for i in range(size)])


def swap(value):
    return lax.ppermute(value, "depth", [(0, 1), (1, 0)])


def divisor(count, wanted):
    while count % wanted:
        wanted -= 1
    return wanted


def piece_sizes(count):
    if count == 12:
        return [1, 7, 4], [(0, 2), (2, 3)]
    return ([1, count - 1] if count > 1 else [1]), [(0, 2)]


def parts_of(own, swapped, offset, gone, back, turn):
    far = [((2,), (3,)), ((3,), (2,))]
    if turn:
        far.reverse()
    return [(own, 0, (0,), (1,)), (swapped, offset, (1,), (0,)), (gone, 0, *far[0]), (back, 0, *far[1])]


def plain_parts(arrays, size):
    even, odd = tuple(range(0, size, 2)), tuple(range(1, size, 2))
    return [(arrays[0], 0, even, odd), (arrays[1], 0, odd, even)]


def on_device(covariance):
    rows = lax.axis_size("row")
    cols = lax.axis_size("col")
    row, col, depth = (lax.axis_index(name) for name in ("row", "col", "depth"))
    place = jnp.stack([row, col, depth]).astype(jnp.int32)
    tile_rows, _, tile_cols, _, tile, _ = covariance.shape
    half = tile // 2
    zero = jnp.zeros((), jnp.int32)
    start = depth.astype(jnp.int32) * half

    def left(first, count):
        where = (zero + first, zero, zero, zero, start, zero)
        return lax.dynamic_slice(covariance, where, (count, 1, 1, 1, half, tile)).reshape(count, half, tile)

    def top(first, count):
        where = (zero, zero, zero + first, zero, start, zero)
        return lax.dynamic_slice(covariance, where, (1, 1, count, 1, half, tile)).reshape(count, half, tile)

    sizes, groups_at = piece_sizes(tile_rows)
    tall = cols == 4 and len(sizes) == 3
    mine = [left(sum(sizes[:i]), size) for i, size in enumerate(sizes)]
    turns = [i % 2 for i in range(len(sizes))]
    pairs = [(0, 1)], [(2, 3)]
    if tall:
        gone = [outward(mine[0], "col")]
        first_parts = parts_of(mine[0], exchange(mine[0], "col", pairs[0]), 0, gone[0], exchange(gone[0], "col", pairs[1]), 0)
    else:
        first_parts = plain_parts(held_and_across(mine[0], "col", cols), cols)

    top_parts = 2 if tile_cols % 2 == 0 else 1
    per_part = tile_cols // top_parts
    tops_held = [spread(top(0, per_part), row, rows)]
    pair = jnp.concatenate([pick(first_parts, side, col) for side in range(2)], 0)
    seed = spread(after(pair, tops_held[0]), row, rows)
    for part in range(1, top_parts):
        tops_held.append(spread(after(top(part * per_part, per_part), seed), row, rows))
    seed_across = cross(seed, rows)
    tops_across = [cross(after(tops_held[0], seed_across), rows)]
    seed_parts = [seed, seed_across, swap(seed), swap(seed_across)]
    if tall:
        gone.append(outward(after(mine[1], pair), "col", turns[1]))
    matrix, inv = factor_start(place, seed_parts, half)
    stages = [matrix]
    for begin, end in ((half, tile), (tile, 2 * tile)):
        matrix, inv = factor_next(matrix, inv, begin, end, half)
        stages.append(matrix)
    for part in range(1, top_parts):
        tops_across.append(cross(after(tops_held[part], stages[part - 1]), rows))
    pieces = []
    for part in range(top_parts):
        waits = stages[2 * min(part, 1)]
        pieces += [
            tops_held[part],
            tops_across[part],
            swap(after(tops_held[part], waits)),
            swap(after(tops_across[part], waits)),
        ]
    groups = [(sizes[0], first_parts)]
    if tall:
        arrived = after(gone[1], stages[2])
        gone.append(outward(after(mine[2], arrived), "col", turns[2]))
        first, second = (0, 3), (1, 2)
        held = jnp.where(col < 2, mine[1], arrived)
        across = exchange(held, "col", pairs[0] + pairs[1])
        groups.append((sizes[1], [(held, 0, first, second), (across, 0, second, first)]))
        pieces[0] = after(pieces[0], held)
    else:
        for number in range(1, len(sizes)):
            groups.append((sizes[number], plain_parts(held_and_across(mine[number], "col", cols), cols)))
    tops = columns(place, inv, pieces, top_parts, divisor(per_part, 2))
    if tall:
        arrived = after(gone[2], tops[1], across)
        first, second = (0, 2), (1, 3)
        held = jnp.where(col < 2, mine[2], arrived)
        across = exchange(held, "col", pairs[0] + pairs[1])
        groups.append((sizes[2], [(held, 0, first, second), (across, 0, second, first)]))
        groups[0] = (sizes[0], [(after(first_parts[0][0], held), *first_parts[0][1:]), *first_parts[1:]])
    out = None
    group = divisor(tile_cols, 2)
    for begin, end in groups_at:
        first_tile = sum(sizes[:begin])
        out = update(place, inv, groups[begin:end], tops, covariance, out, first_tile, group)
    return out


def solution(mesh):
    in_specs = (P(None, "row", None, "col", None, None),)
    out_specs = P(None, "row", None, "col", "depth", None)
    return jax.shard_map(
        on_device, mesh=mesh, in_specs=in_specs, out_specs=out_specs, check_vma=False
    )
```

```python
import functools

import jax
import jax.numpy as jnp
from jax import lax
from jax.experimental import pallas as pl
from jax.experimental.pallas import tpu as pltpu
from jax.sharding import PartitionSpec as P

EXACT = lax.Precision.HIGHEST
F32 = jnp.float32
BF16 = jnp.bfloat16
LIMIT = 56 << 20
ANY = pl.BlockSpec(memory_space=pl.ANY)
LIGHT = pl.CostEstimate(flops=1, bytes_accessed=1, transcendentals=0)
HEAVY = pl.CostEstimate(flops=10**10, bytes_accessed=1, transcendentals=0)


def dot(a, b, ca=1, cb=0, precision=None):
    return lax.dot_general(
        a, b, (((ca,), (cb,)), ((), ())), precision=precision, preferred_element_type=F32
    )


def split(value):
    high = value.astype(BF16)
    return high, (value - high.astype(F32)).astype(BF16)


def diag_inverse(block, n, group=8):
    row_ids = lax.broadcasted_iota(jnp.int32, (n, n), 0)
    col_ids = lax.broadcasted_iota(jnp.int32, (n, n), 1)
    unit = jnp.where(row_ids == col_ids, 1.0, 0.0).astype(F32)
    sub = lax.broadcasted_iota(jnp.int32, (group, n), 0)
    count = n // group
    rows = [block[group * g : group * (g + 1)] for g in range(count)]
    inverse = [unit[group * g : group * (g + 1)] for g in range(count)]

    def lanes(value, index):
        return jnp.broadcast_to(value[:, index : index + 1], (group, n))

    def subs(value, index):
        return jnp.broadcast_to(value[index : index + 1], (group, n))

    done = []
    for g in range(count):
        first = group * g
        here, inv_here = rows[g], inverse[g]
        cols = [lanes(here, first + j) for j in range(group)]
        recips, pivots, inv_pivots, cross = [], [], [], {}
        scale = jnp.zeros((group, n), F32)
        for j in range(group):
            root = lax.rsqrt(subs(cols[j], j))
            recip = root * root
            scale = jnp.where(sub == j, root, scale)
            pivot, inv_pivot = subs(here, j), subs(inv_here, j)
            factor = jnp.where(sub > j, cols[j] * recip, 0.0)
            for later in range(j + 1, group):
                cross[j, later] = subs(cols[later], j)
                cols[later] = cols[later] - factor * cross[j, later]
            here = here - factor * pivot
            inv_here = inv_here - factor * inv_pivot
            recips.append(recip)
            pivots.append(pivot)
            inv_pivots.append(inv_pivot)
        done.append(inv_here * scale)
        for below in range(g + 1, count):
            value, inv_value = rows[below], inverse[below]
            cols = [lanes(value, first + j) for j in range(group)]
            for j in range(group):
                factor = cols[j] * recips[j]
                for later in range(j + 1, group):
                    cols[later] = cols[later] - factor * cross[j, later]
                value = value - factor * pivots[j]
                inv_value = inv_value - factor * inv_pivots[j]
            rows[below], inverse[below] = value, inv_value
    return jnp.concatenate(done, 0)


def factor_steps(matrix, out, start, stop, step):
    n = matrix.shape[0]
    for a in range(start, stop, step):
        e = a + step
        inv = diag_inverse(matrix[a:e, a:e], step)
        if a:
            out[a:e, :a] = dot(inv, out[a:e, :a], precision=EXACT)
        out[a:e, a:e] = inv
        if e < n:
            panel = dot(inv, matrix[a:e, e:], precision=EXACT)
            matrix[e:, e:] = matrix[e:, e:] - dot(panel, panel, 0, 0, EXACT)
            out[e:, :e] = out[e:, :e] - dot(panel, out[a:e, :e], 0, 0, EXACT)


def assemble_kernel(place, mine, across, mine_other, across_other, matrix, out, *, step):
    half = mine.shape[1]
    tile = mine.shape[2]
    parity = lax.rem(place[0], 2)
    depth = place[2]
    for ref, tile_row, side in (
        (mine, parity, depth),
        (across, 1 - parity, depth),
        (mine_other, parity, 1 - depth),
        (across_other, 1 - parity, 1 - depth),
    ):
        start = pl.multiple_of(tile_row * tile + side * half, half)
        for q in range(2):
            matrix[pl.ds(start, half), q * tile : (q + 1) * tile] = ref[q]
    out[...] = jnp.zeros_like(out)
    factor_steps(matrix, out, 0, step, step)


def eliminate_kernel(matrix_in, inv_in, matrix, inv, *, start, stop, step):
    matrix[...] = matrix_in[...]
    inv[...] = inv_in[...]
    factor_steps(matrix, inv, start, stop, step)


def factor_start(place, pieces, step):
    n = 2 * pieces[0].shape[-1]
    whole = pl.BlockSpec(memory_space=pltpu.VMEM)
    square = jax.ShapeDtypeStruct((n, n), F32)
    return pl.pallas_call(
        functools.partial(assemble_kernel, step=step),
        out_shape=[square, square],
        in_specs=[pl.BlockSpec(memory_space=pltpu.SMEM)] + [whole] * 4,
        out_specs=[whole] * 2,
        compiler_params=pltpu.CompilerParams(vmem_limit_bytes=16 << 20),
        cost_estimate=LIGHT,
        name="factor_start",
    )(place, *pieces)


def factor_next(matrix, inv, start, stop, step):
    n = matrix.shape[0]
    whole = pl.BlockSpec(memory_space=pltpu.VMEM)
    square = jax.ShapeDtypeStruct((n, n), F32)
    return pl.pallas_call(
        functools.partial(eliminate_kernel, start=start, stop=stop, step=step),
        out_shape=[square, square],
        in_specs=[whole] * 2,
        out_specs=[whole] * 2,
        compiler_params=pltpu.CompilerParams(vmem_limit_bytes=16 << 20),
        cost_estimate=HEAVY if stop == n else LIGHT,
        name="factor_next",
    )(matrix, inv)


def columns_kernel(place, inv, *refs, parts):
    both_parts, first, raw = refs[-3:]
    group, half, tile = refs[0].shape
    n = 2 * tile
    parity = lax.rem(place[0], 2)
    depth = place[2]
    turn = pl.program_id(0) // (pl.num_programs(0) // parts)
    sides = ((parity, depth), (1 - parity, depth), (parity, 1 - depth), (1 - parity, 1 - depth))

    for part in range(parts):

        @pl.when(turn == part)
        def _(part=part):
            for ref, (q, side) in zip(refs[4 * part : 4 * part + 4], sides):
                start = pl.multiple_of(q * tile + side * half, half)
                for b in range(group):
                    raw[pl.ds(start, half), b * tile : (b + 1) * tile] = ref[b]

    for b in range(group):
        here = slice(b * tile, (b + 1) * tile)
        for start, stop in ((0, tile), (tile, n)):
            total = dot(inv[start:stop, :stop], raw[:stop, here], precision=EXACT)
            if start == 0:
                first[:, here] = jnp.broadcast_to(total[:1], (8, tile))
                total = jnp.where(lax.broadcasted_iota(jnp.int32, total.shape, 0) == 0, 0.0, total)
            high, low = split(total)
            both_parts[start:stop, here] = high
            both_parts[n + start : n + stop, here] = low


def columns(place, inv, pieces, parts, group):
    count, half, tile = pieces[0].shape
    n = 2 * tile
    steps = count // group
    width = group * tile

    def piece(part):
        return pl.BlockSpec(
            (group, half, tile), lambda j, place: (jnp.clip(j - part * steps, 0, steps - 1), 0, 0)
        )

    return pl.pallas_call(
        functools.partial(columns_kernel, parts=parts),
        out_shape=[
            jax.ShapeDtypeStruct((2 * n, parts * count * tile), BF16),
            jax.ShapeDtypeStruct((8, parts * count * tile), F32),
        ],
        grid_spec=pltpu.PrefetchScalarGridSpec(
            num_scalar_prefetch=1,
            grid=(parts * steps,),
            in_specs=[pl.BlockSpec((n, n), lambda j, place: (0, 0))]
            + [piece(number // 4) for number in range(len(pieces))],
            out_specs=[
                pl.BlockSpec((2 * n, width), lambda j, place: (0, j)),
                pl.BlockSpec((8, width), lambda j, place: (0, j)),
            ],
            scratch_shapes=[pltpu.VMEM((n, width), F32)],
        ),
        compiler_params=pltpu.CompilerParams(vmem_limit_bytes=LIMIT),
        cost_estimate=HEAVY,
        name="columns",
    )(place, inv, *pieces)


def update_kernel(place, inv, *refs, sources, plan, first_tile):
    cands = refs[:sources]
    top, top_first, tiles = refs[sources : sources + 3]
    out, raw, exact, lead, high, low = refs[-6:]
    chunk_rows, _, group, _, half, tile = out.shape
    n = 2 * tile
    step = pl.program_id(0)
    row, col = place[0], place[1]

    @pl.when(step == 0)
    def _():
        for number, offset, at_first, at_second, begin, size in plan:
            ref = cands[number]
            place_rows = slice(begin * half, (begin + size) * half)
            for at, lanes in ((at_first, slice(0, tile)), (at_second, slice(tile, n))):
                here = functools.reduce(jnp.logical_or, [col == index for index in at])

                @pl.when(here)
                def _(ref=ref, lanes=lanes, place_rows=place_rows, offset=offset, size=size):
                    raw[place_rows, lanes] = ref[offset : offset + size].reshape(size * half, tile)

        for start, stop in ((0, tile), (tile, n)):
            total = dot(raw[:, :stop], inv[start:stop, :stop], 1, 1, EXACT)
            exact[:, start:stop] = total
            if start == 0:
                lead[...] = jnp.broadcast_to(total[:, :1], lead.shape)
            high[:, start:stop], low[:, start:stop] = split(total)

    leads = jnp.concatenate([lead[...]] * (tile // 128), 1)
    for b in range(group):
        here = slice(b * tile, (b + 1) * tile)
        total = dot(high[...], top[:n, here])
        total += dot(high[...], top[n:, here])
        total += dot(low[...], top[:n, here])
        total += leads * top_first[:1, here]
        for a in range(chunk_rows):
            out[a, 0, b, 0] = tiles[a, 0, b, 0] - total[a * half : (a + 1) * half]

    @pl.when(jnp.logical_and(first_tile == 0, row < 2))
    def _():
        out[0] = jnp.zeros(out.shape[1:], F32)

    @pl.when(jnp.logical_and(step == 0, col < 2))
    def _():
        start = pl.multiple_of(jnp.minimum(col, 1) * tile, tile)
        panel = exact[:, pl.ds(start, tile)]
        for a in range(chunk_rows):
            out[a, 0, 0, 0] = panel[a * half : (a + 1) * half]


def update(place, inv, groups, top, covariance, before, first_tile, group):
    tile_rows, _, tile_cols, _, tile, _ = covariance.shape
    half = tile // 2
    n = 2 * tile
    cands, plan = [], []
    begin = 0
    for size, parts in groups:
        for array, offset, at_first, at_second in parts:
            number = next((i for i, known in enumerate(cands) if known is array), len(cands))
            if number == len(cands):
                cands.append(array)
            plan.append((number, offset, at_first, at_second, begin, size))
        begin += size
    chunk_rows = begin
    rows = chunk_rows * half
    width = group * tile
    chunk = first_tile // chunk_rows
    in_specs = [pl.BlockSpec((n, n), lambda j, place: (0, 0))]
    in_specs += [pl.BlockSpec(array.shape, lambda j, place: (0, 0, 0)) for array in cands]
    in_specs += [
        pl.BlockSpec((2 * n, width), lambda j, place: (0, j)),
        pl.BlockSpec((8, width), lambda j, place: (0, j)),
        pl.BlockSpec(
            (chunk_rows, 1, group, 1, half, tile),
            lambda j, place: (chunk, 0, j, 0, place[2], 0),
        ),
    ]
    operands = [place, inv, *cands, *top, covariance]
    aliases = {}
    if before is not None:
        in_specs.append(ANY)
        aliases = {len(operands): 0}
        operands.append(before)
    return pl.pallas_call(
        functools.partial(update_kernel, sources=len(cands), plan=plan, first_tile=first_tile),
        out_shape=jax.ShapeDtypeStruct((tile_rows, 1, tile_cols, 1, half, tile), F32),
        grid_spec=pltpu.PrefetchScalarGridSpec(
            num_scalar_prefetch=1,
            grid=(tile_cols // group,),
            in_specs=in_specs,
            out_specs=pl.BlockSpec(
                (chunk_rows, 1, group, 1, half, tile), lambda j, place: (chunk, 0, j, 0, 0, 0)
            ),
            scratch_shapes=[
                pltpu.VMEM((rows, n), F32),
                pltpu.VMEM((rows, n), F32),
                pltpu.VMEM((rows, 128), F32),
                pltpu.VMEM((rows, n), BF16),
                pltpu.VMEM((rows, n), BF16),
            ],
        ),
        input_output_aliases=aliases,
        compiler_params=pltpu.CompilerParams(vmem_limit_bytes=LIMIT),
        cost_estimate=pl.CostEstimate(
            flops=12 * rows * n * tile_cols * tile,
            bytes_accessed=8 * rows * tile_cols * tile,
            transcendentals=0,
        ),
        name="update",
    )(*operands)


def after(value, *earlier):
    return lax.optimization_barrier((value, *earlier))[0] if earlier else value


def outward(value, axis, turn=0):
    return lax.ppermute(value, axis, [(0, 3), (1, 2)] if turn else [(0, 2), (1, 3)])


def exchange(value, axis, pairs):
    return lax.ppermute(value, axis, pairs + [(j, i) for i, j in pairs])


def held_and_across(value, axis, size):
    held = value
    index = lax.axis_index(axis)
    step = 2
    while step < size:
        pairs = [(i, i + step) for i in range(step) if i + step < size]
        got = lax.ppermute(held, axis, pairs)
        held = jnp.where((index >= step) & (index < 2 * step), got, held)
        step *= 2
    return held, lax.ppermute(held, axis, [(i, i ^ 1) for i in range(size)])


def pick(parts, side, index):
    value = parts[-1][0]
    for array, _, *at in parts[:-1]:
        here = functools.reduce(jnp.logical_or, [index == position for position in at[side]])
        value = jnp.where(here, array, value)
    return value


def spread(value, index, size):
    held = value
    step = 2
    while step < size:
        pairs = [(i, i + step) for i in range(step) if i + step < size]
        got = lax.ppermute(held, "row", pairs)
        held = jnp.where((index >= step) & (index < 2 * step), got, held)
        step *= 2
    return held


def cross(value, size):
    return lax.ppermute(value, "row", [(i, i ^ 1) for i in range(size)])


def swap(value):
    return lax.ppermute(value, "depth", [(0, 1), (1, 0)])


def divisor(count, wanted):
    while count % wanted:
        wanted -= 1
    return wanted


def piece_sizes(count):
    if count == 12:
        return [1, 5, 6], [(0, 2), (2, 3)]
    return ([1, count - 1] if count > 1 else [1]), [(0, 2)]


def parts_of(own, swapped, offset, gone, back, turn):
    far = [((2,), (3,)), ((3,), (2,))]
    if turn:
        far.reverse()
    return [(own, 0, (0,), (1,)), (swapped, offset, (1,), (0,)), (gone, 0, *far[0]), (back, 0, *far[1])]


def plain_parts(arrays, size):
    even, odd = tuple(range(0, size, 2)), tuple(range(1, size, 2))
    return [(arrays[0], 0, even, odd), (arrays[1], 0, odd, even)]


def on_device(covariance):
    rows = lax.axis_size("row")
    cols = lax.axis_size("col")
    row, col, depth = (lax.axis_index(name) for name in ("row", "col", "depth"))
    place = jnp.stack([row, col, depth]).astype(jnp.int32)
    tile_rows, _, tile_cols, _, tile, _ = covariance.shape
    half = tile // 2
    zero = jnp.zeros((), jnp.int32)
    start = depth.astype(jnp.int32) * half

    def left(first, count):
        where = (zero + first, zero, zero, zero, start, zero)
        return lax.dynamic_slice(covariance, where, (count, 1, 1, 1, half, tile)).reshape(count, half, tile)

    def top(first, count):
        where = (zero, zero, zero + first, zero, start, zero)
        return lax.dynamic_slice(covariance, where, (1, 1, count, 1, half, tile)).reshape(count, half, tile)

    sizes, groups_at = piece_sizes(tile_rows)
    tall = cols == 4 and len(sizes) == 3
    mine = [left(sum(sizes[:i]), size) for i, size in enumerate(sizes)]
    turns = [i % 2 for i in range(len(sizes))]
    pairs = [(0, 1)], [(2, 3)]
    if tall:
        gone = [outward(mine[0], "col")]
        first_parts = parts_of(mine[0], exchange(mine[0], "col", pairs[0]), 0, gone[0], exchange(gone[0], "col", pairs[1]), 0)
    else:
        first_parts = plain_parts(held_and_across(mine[0], "col", cols), cols)

    top_parts = 2 if tile_cols % 2 == 0 else 1
    per_part = tile_cols // top_parts
    tops_held = [spread(top(0, per_part), row, rows)]
    pair = jnp.concatenate([pick(first_parts, side, col) for side in range(2)], 0)
    seed = spread(after(pair, tops_held[0]), row, rows)
    for part in range(1, top_parts):
        tops_held.append(spread(after(top(part * per_part, per_part), seed), row, rows))
    seed_across = cross(seed, rows)
    tops_across = [cross(after(tops_held[0], seed_across), rows)]
    seed_parts = [seed, seed_across, swap(seed), swap(seed_across)]
    if tall:
        gone.append(outward(after(mine[1], pair), "col", turns[1]))
    matrix, inv = factor_start(place, seed_parts, half)
    stages = [matrix]
    for begin, end in ((half, tile), (tile, 2 * tile)):
        matrix, inv = factor_next(matrix, inv, begin, end, half)
        stages.append(matrix)
    for part in range(1, top_parts):
        tops_across.append(cross(after(tops_held[part], stages[part - 1]), rows))
    pieces = []
    for part in range(top_parts):
        waits = stages[2 * min(part, 1)]
        pieces += [
            tops_held[part],
            tops_across[part],
            swap(after(tops_held[part], waits)),
            swap(after(tops_across[part], waits)),
        ]
    groups = [(sizes[0], first_parts)]
    if tall:
        arrived = after(gone[1], stages[2])
        gone.append(outward(after(mine[2], arrived), "col", turns[2]))
        first, second = (0, 3), (1, 2)
        held = jnp.where(col < 2, mine[1], arrived)
        across = exchange(held, "col", pairs[0] + pairs[1])
        groups.append((sizes[1], [(held, 0, first, second), (across, 0, second, first)]))
        pieces[0] = after(pieces[0], held)
    else:
        for number in range(1, len(sizes)):
            groups.append((sizes[number], plain_parts(held_and_across(mine[number], "col", cols), cols)))
    tops = columns(place, inv, pieces, top_parts, divisor(per_part, 2))
    if tall:
        arrived = after(gone[2], tops[1], across)
        first, second = (0, 2), (1, 3)
        held = jnp.where(col < 2, mine[2], arrived)
        across = exchange(held, "col", pairs[0] + pairs[1])
        groups.append((sizes[2], [(held, 0, first, second), (across, 0, second, first)]))
        groups[0] = (sizes[0], [(after(first_parts[0][0], held), *first_parts[0][1:]), *first_parts[1:]])
    out = None
    group = divisor(tile_cols, 2)
    for begin, end in groups_at:
        first_tile = sum(sizes[:begin])
        out = update(place, inv, groups[begin:end], tops, covariance, out, first_tile, group)
    return out


def solution(mesh):
    in_specs = (P(None, "row", None, "col", None, None),)
    out_specs = P(None, "row", None, "col", "depth", None)
    return jax.shard_map(
        on_device, mesh=mesh, in_specs=in_specs, out_specs=out_specs, check_vma=False
    )
```
